256 devices in a mesh: ia: 8 (over y, core), ja: 32 (over x, z).
Axes of the slice: x: 4, y: 4, z: 8, core: 2. Of those that a mesh axis runs over, the one named last changes fastest.
Arguments:
- position: float32 [3, 1048576], P(None, ('ia', 'ja')), may hold values from -6 to 6
- velocity: float32 [3, 1048576], P(None, ('ia', 'ja')), may hold values from -4 to 4
- acceleration: float32 [3, 1048576], P(None, ('ia', 'ja')), may hold values from -4 to 4
- old_jerk: float32 [3, 1048576], P(None, ('ia', 'ja')), may hold values from -6 to 6
- star_mass: float32 [1048576], P(('ia', 'ja')), may hold values from 6.6757204e-09 to 6.67572e-06
- elapsed: float32 [1048576], P(('ia', 'ja')), may hold values from 0.05 to 1
- active: int32 [4096], P('ia'), may hold values from 0 to 1048575, as said below
Outputs:
- corrected: float32 [12, 4096], P(None, 'ia')
- potential: float32 [4096], P('ia')
The draws below stay inside these ranges and needn't reach their ends.
Inputs may be any that keep to these rules, and one draw needn't show every extreme that they name: `active`: 4096 distinct star indices.
All inputs are finite; a program needn't handle non-finite values.
Results may differ from the reference program's by a relative error of at most 0.0003.
Values sent between devices are 32-bit elements; how exact they have to be, the bound alone decides.
A program may use at most 64 MiB of HBM per device.

```python
import math
import jax
import jax.numpy as jnp
from jax import lax

STAR_DEV = 4096
STAR_COUNT = 1048576
ACTIVE_COUNT = 4096
N_JA = 32


def draw_active(key, part):
    key = jax.random.fold_in(key, 7)
    first_key, key_second, third_key = jax.random.split(key, 3)
    reward_per_unit = (1 << 20) * ACTIVE_COUNT // STAR_COUNT
    baseline_score = jax.random.randint(first_key, (STAR_COUNT,), 0, 1 << 20)
    extra_reward = jax.random.randint(key_second, (N_JA,), 0, 4) * reward_per_unit
    column_entry = jnp.arange(STAR_COUNT, dtype=jnp.int32) // STAR_DEV % N_JA
    score_total = baseline_score + extra_reward[column_entry]
    order = jnp.argsort(-score_total, stable=True)[:ACTIVE_COUNT]
    mixed = jax.random.permutation(third_key, order)
    return mixed.astype(jnp.int32)


def block_levels(rng, shape, cuts, smallest, largest):
    def one(dim, shards_of):
        steps = jax.random.uniform(jax.random.fold_in(jax.random.fold_in(rng, 6), dim), (shards_of,), jnp.float32, smallest / len(cuts), largest / len(cuts))
        return jnp.repeat(jnp.exp(steps), shape[dim] // shards_of).reshape((-1,) + (1,) * (len(shape) - dim - 1))

    loudness = one(*cuts[0])
    for cut in cuts[1:]:
        loudness = loudness * one(*cut)
    return loudness


def scatter_about(rng, dims, scale, reach, cuts=(), held_as=jnp.bfloat16):
    entries = jax.random.normal(rng, dims, jnp.float32) * scale
    if len(cuts) > 0:
        entries = block_levels(rng, dims, cuts, -0.22, 0.18) * entries
    return jnp.clip(entries, min=-reach, max=reach).astype(held_as)


def setup_inputs(seed: int = 0) -> dict:
    keys = jax.random.split(jax.random.key(seed), 8)
    return {
        "position": scatter_about(keys[0], (3, STAR_COUNT), 1.0, 6.0, ((1, 256),), jnp.float32),
        "velocity": scatter_about(keys[1], (3, STAR_COUNT), 0.5, 4.0, ((1, 256),), jnp.float32),
        "acceleration": scatter_about(keys[2], (3, STAR_COUNT), 0.5, 4.0, ((1, 256),), jnp.float32),
        "old_jerk": scatter_about(keys[3], (3, STAR_COUNT), 1.0, 6.0, ((1, 256),), jnp.float32),
        "star_mass": jnp.clip(jnp.exp(math.log(6.67572021484375e-06) - 6.9077552 * jax.random.uniform(keys[4], (STAR_COUNT,), jnp.float32) ** block_levels(keys[4], (STAR_COUNT,), ((0, 256),), -0.2, 0.2)), 6.675720420901143e-09, 6.67572021484375e-06),
        "elapsed": jnp.clip(jnp.exp(math.log(1.0) - 2.9957323 * jax.random.uniform(keys[5], (STAR_COUNT,), jnp.float32) ** block_levels(keys[5], (STAR_COUNT,), ((0, 256),), -0.2, 0.2)), 0.05, 1.0),
        "active": draw_active(jax.random.fold_in(keys[7], 71), 0),
    }


soft_square = 0.0001

def predict(position, velocity, acceleration, old_jerk, elapsed):
    span = elapsed[None, :]
    pos_pred = position + span * (velocity + span * (acceleration / 2.0 + span * old_jerk / 6.0))
    vel_pred = velocity + span * (acceleration + span * old_jerk / 2.0)
    return (pos_pred, vel_pred)

def interact(target_pos, target_vel, target_ids, field, field_ids):
    rows = target_pos.shape[1]
    width = field.shape[1]
    block_width = min(width, max(128, 262144 // rows))
    if width % block_width != 0:
        block_width = width
    count = width // block_width

    def step_block(index, totals):
        block = lax.dynamic_slice_in_dim(field, index * block_width, block_width, 1)
        block_ids = lax.dynamic_slice_in_dim(field_ids, index * block_width, block_width, 0)
        offset = block[0:3, None, :] - target_pos[:, :, None]
        relvel = block[3:6, None, :] - target_vel[:, :, None]
        dist = lax.optimization_barrier(jnp.sum(offset * offset, 0)) + soft_square
        inv_root = lax.rsqrt(dist)
        distinct = block_ids[None, :] != target_ids[:, None]
        weight = jnp.where(distinct, block[6][None, :] * inv_root, 0.0)
        inv_square = inv_root * inv_root
        cube = weight * inv_square
        along = 3.0 * lax.optimization_barrier(jnp.sum(offset * relvel, 0)) * inv_square
        accel_sum = lax.optimization_barrier(jnp.sum(cube[None] * offset, 2))
        jerk_sum = lax.optimization_barrier(jnp.sum(cube[None] * (relvel - along[None] * offset), 2))
        return (totals[0] + accel_sum, totals[1] + jerk_sum, totals[2] - lax.optimization_barrier(jnp.sum(weight, 1)))
    start = (jnp.zeros((3, rows), jnp.float32), jnp.zeros((3, rows), jnp.float32), jnp.zeros((rows,), jnp.float32))
    return lax.fori_loop(0, count, step_block, start)

def correct(state, span, accel_new, jerk_new):
    pos_now = state[0:3]
    vel_now = state[3:6]
    accel_old = state[6:9]
    jerk_prev = state[9:12]
    times = span[None, :]
    accel_gap = accel_old - accel_new
    second_term = -6.0 * accel_gap - times * (4.0 * jerk_prev + 2.0 * jerk_new)
    third_term = 12.0 * accel_gap + 6.0 * times * (jerk_prev + jerk_new)
    pos_new = pos_now + times * times * (second_term / 24.0 + third_term / 120.0)
    vel_new = vel_now + times * (second_term / 6.0 + third_term / 24.0)
    return jnp.concatenate([pos_new, vel_new, accel_new, jerk_new], 0)

def reference(position, velocity, acceleration, old_jerk, star_mass, elapsed, active):
    pos_pred, vel_pred = predict(position, velocity, acceleration, old_jerk, elapsed)
    packed = jnp.concatenate([pos_pred, vel_pred, acceleration, old_jerk], 0)
    chosen = jnp.take(packed, active, axis=1)
    spans = jnp.take(elapsed, active)
    field = jnp.concatenate([pos_pred, vel_pred, star_mass[None, :]], 0)
    field_ids = jnp.arange(STAR_COUNT, dtype=jnp.int32)
    groups = ACTIVE_COUNT // 8
    group_pos = chosen[0:3].reshape(3, groups, 8).transpose(1, 0, 2)
    group_vel = chosen[3:6].reshape(3, groups, 8).transpose(1, 0, 2)
    group_ids = active.reshape(groups, 8)

    def one_group(pieces):
        return interact(pieces[0], pieces[1], pieces[2], field, field_ids)
    accel_all, jerk_all, pot_all = lax.map(one_group, (group_pos, group_vel, group_ids))
    accel_new = accel_all.transpose(1, 0, 2).reshape(3, ACTIVE_COUNT)
    jerk_new = jerk_all.transpose(1, 0, 2).reshape(3, ACTIVE_COUNT)
    potential = pot_all.reshape(ACTIVE_COUNT)
    corrected = correct(chosen, spans, accel_new, jerk_new)
    return (corrected, potential)
```

```python
import functools

import jax
import jax.numpy as jnp
import numpy as np
from jax import lax
from jax.experimental import pallas as pl
from jax.experimental.pallas import tpu as pltpu
from jax.sharding import PartitionSpec as P

soft_square = 0.0001
self_root = float(np.float64(np.float32(soft_square)) ** -0.5)
MESH = pl.DeviceIdType.MESH
F32 = jnp.float32
BF16 = jnp.bfloat16

N_IA = 8
N_X = 4
N_Z = 8
CHUNK = 8192


def split_three(value):
    high = value.astype(BF16)
    rest = value - high.astype(F32)
    middle = rest.astype(BF16)
    low = (rest - middle.astype(F32)).astype(BF16)
    return high, middle, low


def place():
    ia = lax.axis_index("ia")
    ja = lax.axis_index("ja")
    return ia, ja, ja // N_Z, ja % N_Z


def enter(peers):
    barrier = pltpu.get_barrier_semaphore()
    for peer in peers:
        pl.semaphore_signal(barrier, inc=1, device_id=peer, device_id_type=MESH)
    pl.semaphore_wait(barrier, len(peers))


def push(src, dst, send_sem, recv_sem, peer):
    return pltpu.make_async_remote_copy(
        src_ref=src, dst_ref=dst, send_sem=send_sem, recv_sem=recv_sem,
        device_id=peer, device_id_type=MESH,
    )


def ja_peers(ia, x, z):
    along_x = [(ia, ((x + d) % N_X) * N_Z + z) for d in range(1, N_X)]
    along_z = [(ia, x * N_Z + (z + d) % N_Z) for d in range(1, N_Z)]
    return along_x, along_z


def wait_all(slots, count, send, recv, peer):
    part = slots.at[pl.ds(0, count)]
    push(part, part, send, recv, peer).wait()


def share_over_ja(x, z, part, along_x, along_z, from_z, full, sems, meanwhile=None):
    from_z[z] = part
    for d in range(1, N_Z):
        push(from_z.at[z], from_z.at[z], sems.at[0], sems.at[1], along_z[d - 1]).start()
    wait_all(from_z, N_Z - 1, sems.at[0], sems.at[1], along_z[0])
    total = from_z[0]
    for i in range(1, N_Z):
        total = total + from_z[i]
    full[x] = total
    for d in range(1, N_X):
        push(full.at[x], full.at[x], sems.at[2], sems.at[3], along_x[d - 1]).start()
    if meanwhile is not None:
        meanwhile()
    wait_all(full, N_X - 1, sems.at[2], sems.at[3], along_x[0])


def gather_kernel(
    pos_in, vel_in, acc_in, jerk_in, mass_in, elapsed_in, active_in,
    state, field,
    pos, vel, acc, jerk, mass, elapsed, active,
    ids, packed, outgoing, incoming, from_z,
    load, id_send, id_recv, part_send, part_recv, field_send, field_recv, ja_sems,
):
    ia, ja, x, z = place()
    y, core = ia // 2, ia % 2
    star_dev = pos.shape[1]
    loads = []
    for i, (src, dst) in enumerate((
        (active_in, active), (pos_in, pos), (vel_in, vel), (acc_in, acc), (jerk_in, jerk),
        (elapsed_in, elapsed), (mass_in, mass),
    )):
        c = pltpu.make_async_copy(src, dst, load.at[i])
        c.start()
        loads.append(c)
    along_x, along_z = ja_peers(ia, x, z)
    along_ia = [((ia + d) % N_IA, ja) for d in range(1, N_IA)]
    plane = [
        ((ia + d) % N_IA, ((x + e) % N_X) * N_Z + z)
        for d in range(N_IA) for e in range(N_X) if d + e > 0
    ]
    enter(plane + along_z)

    loads[0].wait()

    def send_ids(d):
        return push(active, ids.at[ia], id_send.at[d], id_recv.at[d], ((ia + d) % N_IA, ja))

    for d in range(1, N_IA):
        send_ids(d).start()
    ids[ia] = active[...]

    for c in loads[1:]:
        c.wait()
    span = elapsed[...]
    a, j = acc[...], jerk[...]
    packed[0:3, :] = pos[...] + span * (vel[...] + span * (a / 2.0 + span * j / 6.0))
    packed[3:6, :] = vel[...] + span * (a + span * j / 2.0)
    packed[6:7, :] = span
    packed[7:8, :] = mass[...]
    packed[8:11, :] = a
    packed[11:14, :] = j
    packed[14:16, :] = jnp.zeros((2, star_dev), F32)
    mine = packed.at[pl.ds(0, 8)]
    keep = pltpu.make_async_copy(mine, field.at[ia], load.at[7])
    keep.start()

    sister = (y * 2 + 1 - core, ja)
    field_copies = []
    for d in range(1, 4):
        peer = ((((y + d) % 4) * 2 + core), ja)
        c = push(mine, field.at[ia], field_send.at[d], field_recv.at[d], peer)
        c.start()
        field_copies.append(c)
    own_copy = push(mine, field.at[ia], field_send.at[0], field_recv.at[0], sister)
    own_copy.start()

    first = (ia * lax.axis_size("ja") + ja) * star_dev

    def send_part(d, e):
        dest, dest_x = (ia + d) % N_IA, (x + e) % N_X
        return push(
            outgoing.at[dest, dest_x], incoming.at[ia * N_X + x], part_send, part_recv,
            (dest, dest_x * N_Z + z),
        )

    def pick(d, carry):
        dest = (ia + d) % N_IA

        @pl.when(d > 0)
        def _():
            send_ids(N_IA - d).wait_recv()

        for b in range(N_X):
            spot = jnp.broadcast_to(ids[dest, :, 128 * b:128 * b + 128] - first, (8, 128))
            tile, lane = spot >> 7, spot & 127
            found = [jnp.zeros((8, 128), F32)] * 2
            for q in range(star_dev // 128):
                for h in range(2):
                    part = packed[8 * h:8 * h + 8, q * 128:q * 128 + 128]
                    got = jnp.take_along_axis(part, lane, axis=1, mode="promise_in_bounds")
                    found[h] = jnp.where(tile == q, got, found[h])
            for h in range(2):
                outgoing[dest, b, h] = found[h]
        for e in range(1, N_X):
            send_part(d, e).start()

        @pl.when(d > 0)
        def _():
            send_part(d, 0).start()

        return carry

    lax.fori_loop(0, N_IA, pick, 0)
    for d in range(1, N_IA):
        send_ids(d).wait_send()
    incoming[ia * N_X + x] = outgoing[ia, x]

    wait_all(incoming, N_IA * N_X - 1, part_send, part_recv, plane[0])
    total = incoming[0]
    for i in range(1, N_IA * N_X):
        total = total + incoming[i]
    forwards = []

    def hand_on():
        for c in field_copies:
            c.wait()
        for d in range(1, 4):
            origin = ((y + d) % 4) * 2 + core
            c = push(
                field.at[origin], field.at[origin], field_send.at[3 + d], field_recv.at[3 + d], sister
            )
            c.start()
            forwards.append(c)

    share_over_ja(x, z, total, along_x, along_z, from_z, state, ja_sems, hand_on)
    keep.wait()
    own_copy.wait()
    for c in forwards:
        c.wait()


def pair_kernel(state, field_in, sums, field, targets, stars, totals, load):
    blocks, _, width = field.shape
    chunks = stars.shape[0]
    per_chunk = CHUNK // width
    for i in range(blocks):
        pltpu.make_async_copy(field_in.at[i], field.at[i], load.at[i]).start()
    row_blocks = state.shape[0]

    for b in range(row_blocks):
        for j in range(6):
            row = state[b, 0, j:j + 1, :]
            turned = jnp.broadcast_to(row, (128, 128)).T
            for g in range(16):
                targets[b * 16 + g, j] = turned[8 * g:8 * g + 8]

    def prepare(chunk, carry):
        for part in range(per_chunk):
            index = chunk * per_chunk + part
            pltpu.make_async_copy(field_in.at[index], field.at[index], load.at[index]).wait()
            for j, source in enumerate((0, 1, 2, 3, 4, 5, 7)):
                row = field[index, source:source + 1, :]
                stars[chunk, j, :, part * width:(part + 1) * width] = jnp.broadcast_to(row, (8, width))
        return carry

    lax.fori_loop(0, chunks, prepare, 0)

    def group_sums(group, carry):
        here = [targets[group, j] for j in range(6)]

        def step(chunk, sofar):
            out = list(sofar)
            for t in range(CHUNK // 128):
                star = [stars[chunk, j, :, t * 128:t * 128 + 128] for j in range(7)]
                dx = [star[j] - here[j] for j in range(3)]
                du = [star[3 + j] - here[3 + j] for j in range(3)]
                dist = (dx[0] * dx[0] + dx[1] * dx[1]) + (dx[2] * dx[2] + soft_square)
                dot = dx[0] * du[0] + dx[1] * du[1] + dx[2] * du[2]
                root = lax.rsqrt(dist)
                square = pl.reciprocal(dist, approx=True)
                weight = star[6] * root
                cube = weight * square
                along = dot * square
                for j in range(3):
                    pull = cube * dx[j]
                    out[j] = out[j] + pull
                    out[3 + j] = out[3 + j] + cube * du[j]
                    out[6 + j] = out[6 + j] + along * pull
                out[9] = out[9] + weight
            return tuple(out)

        out = lax.fori_loop(0, chunks, step, (jnp.zeros((8, 128), F32),) * 10)
        b, row = group // 16, group % 16
        whole = list(out[0:3]) + [out[3 + j] - 3.0 * out[6 + j] for j in range(3)] + [out[9]]
        for j in range(7):
            totals[b, j, pl.ds(row * 8, 8), :] = whole[j]
        return carry

    lax.fori_loop(0, row_blocks * 16, group_sums, 0)

    for b in range(row_blocks):
        for j in range(7):
            sums[b, j:j + 1, :] = jnp.sum(totals[b, j].T, 0, keepdims=True)
        sums[b, 7:8, :] = jnp.zeros((1, 128), F32)


def finish_kernel(state, sums, corrected, potential, from_x, from_z, sems):
    ia, ja, x, z = place()
    along_x, along_z = ja_peers(ia, x, z)
    enter(along_x + along_z)
    from_z[z] = sums[...]
    for d in range(1, N_Z):
        push(from_z.at[z], from_z.at[z], sems.at[0], sems.at[1], along_z[d - 1]).start()
    wait_all(from_z, N_Z - 1, sems.at[0], sems.at[1], along_z[0])
    total = from_z[0]
    for i in range(1, N_Z):
        total = total + from_z[i]
    from_x[x] = total
    for d in range(1, N_X):
        push(from_x.at[x], from_x.at[x], sems.at[2], sems.at[3], along_x[d - 1]).start()
    wait_all(from_x, N_X - 1, sems.at[2], sems.at[3], along_x[0])
    full = from_x[0]
    for i in range(1, N_X):
        full = full + from_x[i]
    for b in range(N_X):
        lanes = slice(b * 128, b * 128 + 128)
        times = state[b, 0, 6:7, :]
        for j in range(3):
            accel_new = full[b, j:j + 1, :]
            jerk_new = full[b, 3 + j:4 + j, :]
            accel_gap = state[b, 1, j:j + 1, :] - accel_new
            jerk_prev = state[b, 1, 3 + j:4 + j, :]
            second = -6.0 * accel_gap - times * (4.0 * jerk_prev + 2.0 * jerk_new)
            third = 12.0 * accel_gap + 6.0 * times * (jerk_prev + jerk_new)
            corrected[j:j + 1, lanes] = state[b, 0, j:j + 1, :] + times * times * (second / 24.0 + third / 120.0)
            corrected[3 + j:4 + j, lanes] = state[b, 0, 3 + j:4 + j, :] + times * (second / 6.0 + third / 24.0)
            corrected[6 + j:7 + j, lanes] = accel_new
            corrected[9 + j:10 + j, lanes] = jerk_new
        potential[:, lanes] = state[b, 0, 7:8, :] * self_root - full[b, 6:7, :]


def local(position, velocity, acceleration, old_jerk, star_mass, elapsed, active):
    star_dev = position.shape[1]
    vmem = pl.BlockSpec(memory_space=pltpu.VMEM)
    hbm = pl.BlockSpec(memory_space=pltpu.HBM)
    dma = pltpu.SemaphoreType.DMA
    state, field = pl.pallas_call(
        gather_kernel,
        out_shape=(
            jax.ShapeDtypeStruct((N_X, 2, 8, 128), F32),
            jax.ShapeDtypeStruct((N_IA, 8, star_dev), F32),
        ),
        in_specs=[hbm] * 7,
        out_specs=(vmem, hbm),
        scratch_shapes=[
            pltpu.VMEM((3, star_dev), F32),
            pltpu.VMEM((3, star_dev), F32),
            pltpu.VMEM((3, star_dev), F32),
            pltpu.VMEM((3, star_dev), F32),
            pltpu.VMEM((1, star_dev), F32),
            pltpu.VMEM((1, star_dev), F32),
            pltpu.VMEM((1, 512), jnp.int32),
            pltpu.VMEM((N_IA, 1, 512), jnp.int32),
            pltpu.VMEM((16, star_dev), F32),
            pltpu.VMEM((N_IA, N_X, 2, 8, 128), F32),
            pltpu.VMEM((N_IA * N_X, 2, 8, 128), F32),
            pltpu.VMEM((N_Z, 2, 8, 128), F32),
            dma((8,)), dma((8,)), dma((8,)), dma, dma, dma((8,)), dma((8,)), dma((4,)),
        ],
        compiler_params=pltpu.CompilerParams(
            collective_id=0, has_side_effects=True, vmem_limit_bytes=56 << 20
        ),
        name="gather_targets",
    )(
        position, velocity, acceleration, old_jerk, star_mass.reshape(1, -1),
        elapsed.reshape(1, -1), active.reshape(1, -1),
    )
    chunks = N_IA * star_dev // CHUNK
    sums = pl.pallas_call(
        pair_kernel,
        out_shape=jax.ShapeDtypeStruct((N_X, 8, 128), F32),
        in_specs=[vmem, hbm],
        out_specs=vmem,
        scratch_shapes=[
            pltpu.VMEM((N_IA, 8, star_dev), F32),
            pltpu.VMEM((N_X * 16, 6, 8, 128), F32),
            pltpu.VMEM((chunks, 7, 8, CHUNK), F32),
            pltpu.VMEM((N_X, 7, 128, 128), F32),
            dma((N_IA,)),
        ],
        compiler_params=pltpu.CompilerParams(vmem_limit_bytes=60 << 20),
        name="pair_sums",
    )(state, field)
    corrected, potential = pl.pallas_call(
        finish_kernel,
        out_shape=(
            jax.ShapeDtypeStruct((12, 512), F32),
            jax.ShapeDtypeStruct((1, 512), F32),
        ),
        in_specs=[vmem] * 2,
        out_specs=(vmem, vmem),
        scratch_shapes=[
            pltpu.VMEM((N_X, N_X, 8, 128), F32),
            pltpu.VMEM((N_Z, N_X, 8, 128), F32),
            dma((4,)),
        ],
        compiler_params=pltpu.CompilerParams(
            collective_id=1, has_side_effects=True, vmem_limit_bytes=4 << 20
        ),
        name="reduce_and_correct",
    )(state, sums)
    return corrected, potential.reshape(-1)


def solution(mesh):
    placed = (
        P(None, ("ia", "ja")),
        P(None, ("ia", "ja")),
        P(None, ("ia", "ja")),
        P(None, ("ia", "ja")),
        P(("ia", "ja")),
        P(("ia", "ja")),
        P("ia"),
    )
    return jax.shard_map(
        local, mesh=mesh, in_specs=placed, out_specs=(P(None, "ia"), P("ia")), check_vma=False
    )
```
